32 devices in a mesh: groups: 2 (over y), loop: 4 (over x, core), rows: 4 (over z).
Axes of the slice: x: 2, y: 2, z: 4, core: 2. Of those that a mesh axis runs over, the one named last changes fastest.
Arguments:
- image_feats: float32 [4096, 1152], P(('groups', 'loop', 'rows')), parts along dimension 0, may hold values from -1 to 1
- text_feats: float32 [4096, 1152], P(('groups', 'loop', 'rows')), parts along dimension 0, may hold values from -1 to 1
- log_scale: float32 [1], replicated, may hold values from 2 to 2.5
- bias: float32 [1], replicated, may hold values from -10 to -8
Outputs:
- grad_image: float32 [4096, 1152], P(('groups', 'loop', 'rows')), parts along dimension 0
- grad_text: float32 [4096, 1152], P(('groups', 'loop', 'rows')), parts along dimension 0
- scalars: float32 [6], P('groups'), parts along dimension 0
The draws below stay inside these ranges and needn't reach their ends.
There are 2 independent parts, one for each index of `groups`. The reference program is written for one: setup_inputs(seed, part) draws one part's arguments, and reference() takes and returns one part's arrays. A program takes and returns all parts, laid end to end along the dimension named above; an argument that names none is the same for every part. Nothing has to cross between parts.
All inputs are finite; a program needn't handle non-finite values.
Results may differ from the reference program's by a relative error of at most 0.0045.
Values may be sent and summed in bfloat16 or wider, within the bound.
No kernel may reach another device: no remote copies, remote signals or barrier semaphores. Data moves between devices by JAX's collectives and lax.ppermute only.
A program may use at most 64 MiB of HBM per device.

```python
import math
import jax
import jax.numpy as jnp
from jax import lax

D = 1152
ROWS_DEV = 128
BATCH = 2048
N_ROWS = 4


def common_parts(key):
    key_scale, key_dir, key_normal = jax.random.split(key, 3)
    col_scale = jnp.exp(jax.random.uniform(key_scale, (D,), jnp.float32, math.log(0.3), math.log(3.0)))
    direction = jnp.clip(jax.random.normal(key_dir, (D,), jnp.float32), -3.0, 3.0)
    gaussian = jnp.clip(jax.random.normal(key_normal, (BATCH, D), jnp.float32), -4.0, 4.0)
    pair_noise = gaussian
    position = (jnp.arange(BATCH, dtype=jnp.float32) + 0.5) / BATCH
    return (col_scale, direction, pair_noise, position)


def row_scales(key):
    return jnp.exp(jax.random.uniform(key, (BATCH, 1), jnp.float32, math.log(0.003), math.log(0.03)))


def draw_image_feats(key, part):
    shared_weight = 0.7
    col_scale, direction, pair_noise, position = common_parts(key)
    key = jax.random.fold_in(key, 11)
    row_scale = row_scales(key)
    features = row_scale * col_scale * (shared_weight * position[:, None] * direction + pair_noise)
    return jnp.clip(features, -1.0, 1.0)


def draw_text_feats(key, part):
    shared_weight = 0.7
    col_scale, direction, pair_noise, position = common_parts(key)
    key = jax.random.fold_in(key, 12)
    key_row, key_normal = jax.random.split(key, 2)
    row_scale = row_scales(key_row)
    gaussian = jnp.clip(jax.random.normal(key_normal, (BATCH, D), jnp.float32), -4.0, 4.0)
    own_noise = gaussian
    features = row_scale * col_scale * (shared_weight * position[:, None] * direction + 0.7 * pair_noise + 0.7 * own_noise)
    return jnp.clip(features, -1.0, 1.0)


def setup_inputs(seed: int = 0, part: int = 0) -> dict:
    streams_of = jax.random.split(jax.random.key(seed), 5)
    part_keys = jax.random.split(jax.random.fold_in(streams_of[4], part), 5)
    return {
        "image_feats": draw_image_feats(jax.random.fold_in(jax.random.fold_in(streams_of[4], part), 71), part),
        "text_feats": draw_text_feats(jax.random.fold_in(jax.random.fold_in(streams_of[4], part), 71), part),
        "log_scale": jnp.clip(jax.random.uniform(streams_of[2], (1,), jnp.float32, 2.0, 2.5), 2.0, 2.5),
        "bias": jnp.clip(jax.random.uniform(streams_of[3], (1,), jnp.float32, -10.0, -8.0), -10.0, -8.0),
    }


EPSILON = 1e-06

def unit_rows(features):
    inverse = lax.rsqrt(lax.optimization_barrier(jnp.sum(features * features, axis=1, keepdims=True)) + EPSILON)
    return (features * inverse, inverse)

def through_norm(unit, inverse, grad_unit):
    return (grad_unit - unit * lax.optimization_barrier(jnp.sum(unit * grad_unit, axis=1, keepdims=True))) * inverse

def reference(image_feats, text_feats, log_scale, bias):
    image_unit, image_inv = unit_rows(image_feats)
    text_unit, text_inv = unit_rows(text_feats)
    image_low = image_unit.astype(jnp.bfloat16)
    text_low = text_unit.astype(jnp.bfloat16)
    logit_scale = jnp.exp(log_scale[0])
    logit_bias = bias[0]
    block_rows = ROWS_DEV * N_ROWS
    text_ids = lax.broadcasted_iota(jnp.int32, (1, BATCH), 1)

    def one_block(carry, block_index):
        text_acc, totals = carry
        first_row = (block_index * block_rows).astype(jnp.int32)
        image_rows = lax.dynamic_slice_in_dim(image_low, first_row, block_rows, 0)
        scores = lax.dot_general(image_rows, text_low, (((1,), (1,)), ((), ())), preferred_element_type=jnp.float32)
        logits = logit_scale * scores + logit_bias
        image_ids = first_row + lax.broadcasted_iota(jnp.int32, (block_rows, 1), 0)
        label_sign = jnp.where(image_ids == text_ids, 1.0, -1.0).astype(jnp.float32)
        pair_grad = -label_sign * jax.nn.sigmoid(-label_sign * logits)
        block_stats = jnp.stack([-jnp.sum(jax.nn.log_sigmoid(label_sign * logits)), jnp.sum(pair_grad * logit_scale * scores), jnp.sum(pair_grad)])
        grad_low = pair_grad.astype(jnp.bfloat16)
        image_term = logit_scale * jnp.dot(grad_low, text_low, preferred_element_type=jnp.float32)
        text_term = logit_scale * lax.dot_general(grad_low, image_rows, (((0,), (0,)), ((), ())), preferred_element_type=jnp.float32)
        return ((text_acc + text_term, totals + block_stats), image_term)
    start_carry = (jnp.zeros((BATCH, D), jnp.float32), jnp.zeros((3,), jnp.float32))
    (text_grad_unit, totals), image_blocks = lax.scan(one_block, start_carry, jnp.arange(BATCH // block_rows, dtype=jnp.int32))
    image_grad_unit = image_blocks.reshape(BATCH, D)
    scalars = totals / BATCH
    return (through_norm(image_unit, image_inv, image_grad_unit), through_norm(text_unit, text_inv, text_grad_unit), scalars)
```

```python
import jax
import jax.numpy as jnp
from jax import lax
from jax.experimental import pallas as pl
from jax.experimental.pallas import tpu as pltpu
from jax.sharding import PartitionSpec as P

EPSILON = 1e-06
TILE_BLOCKS = 4
VMEM = pl.BlockSpec(memory_space=pltpu.VMEM)
SMEM = pl.BlockSpec(memory_space=pltpu.SMEM)
PARAMS = pltpu.CompilerParams(vmem_limit_bytes=24 * 1024 * 1024)
ROW_DOT = (((1,), (1,)), ((), ()))
COL_DOT = (((0,), (0,)), ((), ()))


def call(kernel, outs, flops, *args, smem=0):
    nbytes = sum(a.size * a.dtype.itemsize for a in (*args, *outs))
    single = len(outs) == 1
    return pl.pallas_call(
        kernel,
        out_shape=outs[0] if single else tuple(outs),
        in_specs=[SMEM] * smem + [VMEM] * (len(args) - smem),
        out_specs=VMEM if single else tuple([VMEM] * len(outs)),
        compiler_params=PARAMS,
        cost_estimate=pl.CostEstimate(flops=flops, bytes_accessed=nbytes, transcendentals=0),
    )(*args)


def normalize_kernel(feats_ref, low_ref):
    feats = feats_ref[...]
    inverse = lax.rsqrt(jnp.sum(feats * feats, axis=1, keepdims=True) + EPSILON)
    low_ref[...] = (feats * inverse).astype(low_ref.dtype)


def normalize(feats):
    out = jax.ShapeDtypeStruct(feats.shape, jnp.bfloat16)
    return call(normalize_kernel, [out], 4 * feats.size, feats)


def tile_kernel(has_own, n_image, n_text, *refs):
    scale_ref, bias_ref = refs[:2]
    images = jnp.concatenate([r[...] for r in refs[2 : 2 + n_image]], axis=0)
    texts = jnp.concatenate([r[...] for r in refs[2 + n_image : 2 + n_image + n_text]], axis=0)
    outs = refs[2 + n_image + n_text :]
    image_outs, text_outs, stats_ref = outs[:n_image], outs[n_image:-1], outs[-1]
    rows = image_outs[0].shape[0]
    scores = lax.dot_general(images, texts, ROW_DOT, preferred_element_type=jnp.float32)
    scaled = scale_ref[0] * scores
    logits = scaled + bias_ref[0]
    if has_own:
        row = lax.broadcasted_iota(jnp.int32, logits.shape, 0)
        col = lax.broadcasted_iota(jnp.int32, logits.shape, 1)
        sign = jnp.where((row == col) & (row < rows), 1.0, -1.0).astype(jnp.float32)
    else:
        sign = jnp.full(logits.shape, -1.0, jnp.float32)
    against = -sign * logits
    small = jnp.exp(-jnp.abs(against))
    above = jnp.where(against >= 0, 1.0, small) / (1.0 + small)
    pair_grad = -sign * above
    loss = jnp.maximum(against, 0.0) + jnp.log1p(small)
    which = lax.broadcasted_iota(jnp.int32, stats_ref.shape, 0)
    stats_ref[...] = jnp.where(
        which == 0,
        jnp.sum(loss),
        jnp.where(which == 1, jnp.sum(pair_grad * scaled), jnp.sum(pair_grad)),
    )
    grad_low = pair_grad.astype(jnp.bfloat16)
    image_grad = jnp.dot(grad_low, texts, preferred_element_type=jnp.float32)
    for i, ref in enumerate(image_outs):
        ref[...] = image_grad[i * rows : (i + 1) * rows].astype(ref.dtype)
    text_grad = lax.dot_general(grad_low, images, COL_DOT, preferred_element_type=jnp.float32)
    for i, ref in enumerate(text_outs):
        ref[...] = text_grad[i * rows : (i + 1) * rows].astype(ref.dtype)


def tile(has_own, scale, bias, images, texts, image_types, text_types):
    shape = images[0].shape
    outs = [jax.ShapeDtypeStruct(shape, t) for t in (*image_types, *text_types)]
    outs.append(jax.ShapeDtypeStruct((8, 128), jnp.float32))
    flops = 6 * len(images) * len(texts) * shape[0] * shape[0] * shape[1]
    n_image, n_text = len(images), len(texts)

    def kernel(*refs):
        tile_kernel(has_own, n_image, n_text, *refs)

    got = call(kernel, outs, flops, scale, bias, *images, *texts, smem=2)
    return got[:n_image], got[n_image:-1], got[-1]


def add_kernel(*refs):
    total = refs[0][...].astype(jnp.float32)
    for ref in refs[1:-1]:
        total = total + ref[...].astype(jnp.float32)
    refs[-1][...] = total.astype(refs[-1].dtype)


def add_low(*parts):
    out = jax.ShapeDtypeStruct(parts[0].shape, jnp.bfloat16)
    return call(add_kernel, [out], parts[0].size * len(parts), *parts)


def finish_kernel(scale_ref, feats_ref, *refs):
    feats = feats_ref[...]
    inverse = lax.rsqrt(jnp.sum(feats * feats, axis=1, keepdims=True) + EPSILON)
    unit = feats * inverse
    total = refs[0][...].astype(jnp.float32)
    for ref in refs[1:-1]:
        total = total + ref[...].astype(jnp.float32)
    grad = scale_ref[0] * total
    refs[-1][...] = (grad - unit * jnp.sum(unit * grad, axis=1, keepdims=True)) * inverse


def finish(scale, feats, parts):
    out = jax.ShapeDtypeStruct(feats.shape, jnp.float32)
    return call(finish_kernel, [out], 10 * feats.size, scale, feats, *parts, smem=1)


class Ranks:
    def __init__(self, mesh):
        loop, rows = mesh.shape["loop"], mesh.shape["rows"]
        core = 2 if loop % 2 == 0 else 1
        low = 2 if rows % 2 == 0 else 1
        self.sizes = {"x": loop // core, "core": core, "high": rows // low, "low": low}

    def shift(self, value, part, steps):
        n = self.sizes[part]
        steps %= n
        if steps == 0:
            return value
        s = self.sizes
        if part in ("x", "core"):
            axis, inner = "loop", s["core"]
            outer = s["x"]
        else:
            axis, inner = "rows", s["low"]
            outer = s["high"]
        pairs = []
        for a in range(outer):
            for b in range(inner):
                if part in ("x", "high"):
                    to = ((a + steps) % n) * inner + b
                else:
                    to = a * inner + (b + steps) % n
                pairs.append((a * inner + b, to))
        return lax.ppermute(value, axis, pairs)


def gather(ranks, own, far, near):
    held = [ranks.shift(own, far, k) for k in range(ranks.sizes[far])]
    return [[ranks.shift(b, near, k) for k in range(ranks.sizes[near])] for b in held]


def scatter(ranks, partial, far, near):
    n_near, n_far = ranks.sizes[near], ranks.sizes[far]
    got = [None] * n_far
    for f in [*range(1, n_far), 0]:
        got[f] = [ranks.shift(partial[f][k], near, -k) for k in range(n_near)]
    sums = [*got[0]]
    for f in range(1, n_far):
        sums.append(ranks.shift(add_low(*got[f]), far, -f))
    return sums


def sum_everywhere(ranks, value):
    for part in ("core", "x", "low", "high"):
        value = sum([ranks.shift(value, part, k) for k in range(1, ranks.sizes[part])], value)
    return value


def solution(mesh):
    ranks = Ranks(mesh)
    batch_devices = mesh.shape["loop"] * mesh.shape["rows"]

    def shards(image_feats, text_feats, log_scale, bias):
        scale = jnp.exp(log_scale)
        image_low = normalize(image_feats)
        text_low = normalize(text_feats)
        images = gather(ranks, image_low, "low", "x")
        texts = gather(ranks, text_low, "high", "core")
        image_keys = [(f, k) for f in range(len(images)) for k in range(len(images[0]))]
        text_keys = [(f, k) for f in range(len(texts)) for k in range(len(texts[0]))]
        image_part, text_part, stats = {}, {}, None
        one_tile = len(image_keys) <= TILE_BLOCKS and len(text_keys) <= TILE_BLOCKS

        def part_type(key):
            wide = key == (0, 0) or not one_tile
            return jnp.float32 if wide else jnp.bfloat16

        for i in range(0, len(image_keys), TILE_BLOCKS):
            for j in range(0, len(text_keys), TILE_BLOCKS):
                ik, tk = image_keys[i : i + TILE_BLOCKS], text_keys[j : j + TILE_BLOCKS]
                image_term, text_term, tile_stats = tile(
                    i == 0 and j == 0,
                    scale,
                    bias,
                    [images[f][k] for f, k in ik],
                    [texts[f][k] for f, k in tk],
                    [part_type(key) for key in ik],
                    [part_type(key) for key in tk],
                )
                for key, term in zip(ik, image_term):
                    image_part[key] = image_part[key] + term if key in image_part else term
                for key, term in zip(tk, text_term):
                    text_part[key] = text_part[key] + term if key in text_part else term
                stats = tile_stats if stats is None else stats + tile_stats

        def nested(part, like):
            return [
                [part[f, k] if (f, k) == (0, 0) else part[f, k].astype(jnp.bfloat16) for k in range(len(like[0]))]
                for f in range(len(like))
            ]

        image_sums = scatter(ranks, nested(image_part, images), "low", "x")
        text_sums = scatter(ranks, nested(text_part, texts), "high", "core")
        stats = sum_everywhere(ranks, stats)
        scalars = stats[:3, 0] / (batch_devices * image_feats.shape[0])
        grad_image = finish(scale, image_feats, image_sums)
        grad_text = finish(scale, text_feats, text_sums)
        return grad_image, grad_text, scalars

    rows_spec = P(("groups", "loop", "rows"), None)
    return jax.shard_map(
        shards,
        mesh=mesh,
        in_specs=(rows_spec, rows_spec, P(), P()),
        out_specs=(rows_spec, rows_spec, P("groups")),
        check_vma=False,
    )
```

```python
import functools

import jax
import jax.numpy as jnp
from jax import lax
from jax.experimental import pallas as pl
from jax.experimental.pallas import tpu as pltpu
from jax.sharding import PartitionSpec as P

EPSILON = 1e-06
TILE_BLOCKS = 4
FIRST = 4 * 10**9
VMEM = pl.BlockSpec(memory_space=pltpu.VMEM)
SMEM = pl.BlockSpec(memory_space=pltpu.SMEM)
PARAMS = pltpu.CompilerParams(vmem_limit_bytes=24 * 1024 * 1024)
ROW_DOT = (((1,), (1,)), ((), ()))
COL_DOT = (((0,), (0,)), ((), ()))
LOW, WIDE = jnp.bfloat16, jnp.float32


def array(shape, dtype):
    return jax.ShapeDtypeStruct(shape, dtype)


def call(kernel, outs, flops, *args, smem=0):
    nbytes = sum(a.size * a.dtype.itemsize for a in (*args, *outs))
    single = len(outs) == 1
    return pl.pallas_call(
        kernel,
        out_shape=outs[0] if single else tuple(outs),
        in_specs=[SMEM] * smem + [VMEM] * (len(args) - smem),
        out_specs=VMEM if single else tuple([VMEM] * len(outs)),
        compiler_params=PARAMS,
        cost_estimate=pl.CostEstimate(flops=flops, bytes_accessed=nbytes, transcendentals=0),
    )(*args)


def normalize_kernel(feats_ref, *refs):
    feats = feats_ref[...]
    inverse = lax.rsqrt(jnp.sum(feats * feats, axis=1, keepdims=True) + EPSILON)
    refs[-1][...] = (feats * inverse).astype(LOW)


def normalize(feats, *others):
    return call(normalize_kernel, [array(feats.shape, LOW)], 4 * feats.size, feats, *others)


def token_kernel(*refs):
    refs[-1][...] = jnp.zeros(refs[-1].shape, WIDE)


def token(*others):
    return call(token_kernel, [array((8, 128), WIDE)], 1024, *others)


def tile_kernel(has_own, n_image, n_text, *refs):
    scale_ref, bias_ref = refs[:2]
    texts = jnp.concatenate([r[...] for r in refs[2 : 2 + n_text]], axis=0)
    images = jnp.concatenate([r[...] for r in refs[2 + n_text : 2 + n_text + n_image]], axis=0)
    outs = refs[-1 - n_image - n_text :]
    image_outs, text_outs, stats_ref = outs[:n_image], outs[n_image:-1], outs[-1]
    own = image_outs[0].shape[0]
    scores = lax.dot_general(images, texts, ROW_DOT, preferred_element_type=WIDE)
    scaled = scale_ref[0] * scores
    logits = scaled + bias_ref[0]
    if has_own:
        row = lax.broadcasted_iota(jnp.int32, logits.shape, 0)
        col = lax.broadcasted_iota(jnp.int32, logits.shape, 1)
        sign = jnp.where((row == col) & (row < own), 1.0, -1.0).astype(WIDE)
    else:
        sign = jnp.full(logits.shape, -1.0, WIDE)
    against = -sign * logits
    small = jnp.exp(-jnp.abs(against))
    above = jnp.where(against >= 0, 1.0, small) / (1.0 + small)
    pair_grad = -sign * above
    loss = jnp.maximum(against, 0.0) + jnp.log1p(small)
    which = lax.broadcasted_iota(jnp.int32, stats_ref.shape, 0)
    stats_ref[...] = jnp.where(
        which == 0,
        jnp.sum(loss),
        jnp.where(which == 1, jnp.sum(pair_grad * scaled), jnp.sum(pair_grad)),
    )
    grad_low = pair_grad.astype(LOW)

    def spread(value, refs):
        at = 0
        for ref in refs:
            rows = ref.shape[0]
            ref[...] = value[at : at + rows].astype(ref.dtype)
            at += rows

    spread(lax.dot_general(grad_low, images, COL_DOT, preferred_element_type=WIDE), text_outs)
    spread(jnp.dot(grad_low, texts, preferred_element_type=WIDE), image_outs)


def tile(has_own, scale, bias, images, texts, image_types, text_types, *others):
    outs = [array(v.shape, t) for v, t in zip((*images, *texts), (*image_types, *text_types))]
    outs.append(array((8, 128), WIDE))
    n_image, n_text = len(images), len(texts)
    rows_i, rows_t = sum(v.shape[0] for v in images), sum(v.shape[0] for v in texts)
    flops = 6 * rows_i * rows_t * images[0].shape[1]
    kernel = functools.partial(tile_kernel, has_own, n_image, n_text)
    got = call(kernel, outs, flops, scale, bias, *texts, *images, *others, smem=2)
    return got[:n_image], got[n_image:-1], got[-1]


def add_kernel(count, *refs):
    total = refs[0][...].astype(WIDE)
    for ref in refs[1:count]:
        total = total + ref[...].astype(WIDE)
    refs[-1][...] = total.astype(refs[-1].dtype)


def add_low(parts, *others):
    kernel = functools.partial(add_kernel, len(parts))
    return call(kernel, [array(parts[0].shape, LOW)], parts[0].size * len(parts), *parts, *others)


def add_wide(parts, *others):
    kernel = functools.partial(add_kernel, len(parts))
    return call(kernel, [array(parts[0].shape, WIDE)], parts[0].size * len(parts), *parts, *others)


def finish_kernel(count, scale_ref, feats_ref, *refs):
    feats = feats_ref[...]
    inverse = lax.rsqrt(jnp.sum(feats * feats, axis=1, keepdims=True) + EPSILON)
    unit = feats * inverse
    total = refs[0][...].astype(WIDE)
    for ref in refs[1:count]:
        total = total + ref[...].astype(WIDE)
    grad = scale_ref[0] * total
    refs[-2][...] = (grad - unit * jnp.sum(unit * grad, axis=1, keepdims=True)) * inverse
    refs[-1][...] = jnp.zeros(refs[-1].shape, WIDE)


def finish(scale, feats, parts, *others, flops=0):
    kernel = functools.partial(finish_kernel, len(parts))
    outs = [array(feats.shape, WIDE), array((8, 128), WIDE)]
    return call(kernel, outs, 10 * feats.size + flops, scale, feats, *parts, *others, smem=1)


def mean_kernel(count, batch, *refs):
    total = refs[0][...]
    for ref in refs[1:count]:
        total = total + ref[...]
    total = total / batch
    for i in range(3):
        refs[-1][i] = total[i, 0]


def mean_stats(batch, parts, *others):
    return pl.pallas_call(
        functools.partial(mean_kernel, len(parts), float(batch)),
        out_shape=array((3,), WIDE),
        in_specs=[VMEM] * (len(parts) + len(others)),
        out_specs=SMEM,
        compiler_params=PARAMS,
    )(*parts, *others)


class Ranks:
    def __init__(self, mesh):
        loop, rows = mesh.shape["loop"], mesh.shape["rows"]
        core = 2 if loop % 2 == 0 else 1
        low = 2 if rows % 2 == 0 else 1
        self.x, self.core, self.high, self.low = loop // core, core, rows // low, low

    def loop_shift(self, value, x=0, core=0):
        pairs = []
        for a in range(self.x):
            for b in range(self.core):
                to = (a + x) % self.x * self.core + (b + core) % self.core
                pairs.append((a * self.core + b, to))
        return lax.ppermute(value, "loop", pairs)

    def rows_shift(self, value, high=0, low=0):
        pairs = []
        for a in range(self.high):
            for b in range(self.low):
                to = (a + high) % self.high * self.low + (b + low) % self.low
                pairs.append((a * self.low + b, to))
        return lax.ppermute(value, "rows", pairs)


def solution(mesh):
    ranks = Ranks(mesh)
    devices = mesh.shape["loop"] * mesh.shape["rows"]

    def shards(image_feats, text_feats, log_scale, bias):
        rows_dev = image_feats.shape[0]
        scale = jnp.exp(log_scale)
        image_low = normalize(image_feats)
        text_low = normalize(text_feats, image_low)

        images = {(0, 0): image_low}
        for low in range(1, ranks.low):
            images[low, 0] = ranks.rows_shift(image_low, low=low)
        for x in range(1, ranks.x):
            images[0, x] = ranks.loop_shift(image_low, x=x)
        first = token(*images.values())
        for low in range(1, ranks.low):
            for x in range(1, ranks.x):
                images[low, x] = ranks.loop_shift(images[low, 0], x=x)
        second = token(first, *images.values())
        texts = {(0, 0): text_low}
        for high in range(1, ranks.high):
            texts[high, 0] = ranks.rows_shift(text_low, high, high)
        for high in range(ranks.high):
            for core in range(1, ranks.core):
                texts[high, core] = ranks.loop_shift(texts[high, 0], core=core)

        image_keys, text_keys = list(images), list(texts)

        def chunks(keys, arrays):
            out, rows = [[]], 0
            for key in keys:
                if rows + arrays[key].shape[0] > TILE_BLOCKS * rows_dev:
                    out.append([])
                    rows = 0
                out[-1].append(key)
                rows += arrays[key].shape[0]
            return out

        image_chunks, text_chunks = chunks(image_keys, images), chunks(text_keys, texts)
        one_tile = len(image_chunks) == 1 and len(text_chunks) == 1
        image_part, text_part, stats = {}, {}, None

        def part_type(key):
            return LOW if one_tile and key[1] != 0 else WIDE

        for i, ik in enumerate(image_chunks):
            for j, tk in enumerate(text_chunks):
                image_term, text_term, tile_stats = tile(
                    i == 0 and j == 0,
                    scale,
                    bias,
                    [images[key] for key in ik],
                    [texts[key] for key in tk],
                    [part_type(key) for key in ik],
                    [part_type(key) for key in tk],
                    second,
                )
                for key, term in zip(ik, image_term):
                    image_part[key] = image_part[key] + term if key in image_part else term
                for key, term in zip(tk, text_term):
                    text_part[key] = text_part[key] + term if key in text_part else term
                stats = tile_stats if stats is None else stats + tile_stats

        def sent(part, key):
            return part[key].astype(LOW)

        stats = [stats, *[ranks.rows_shift(stats, low=k) for k in range(1, ranks.low)]]
        text_sums, totals = [text_part[0, 0]], []
        for high in range(1, ranks.high):
            got = [ranks.loop_shift(sent(text_part, (high, c)), core=-c) for c in range(1, ranks.core)]
            totals.append(add_low([text_part[high, 0], *got], *stats[1:]))
            text_sums.append(ranks.rows_shift(totals[-1], -high, -high))
        for core in range(1, ranks.core):
            text_sums.append(ranks.loop_shift(sent(text_part, (0, core)), core=-core))
        stats = add_wide(stats, *totals)
        steps = [(x, c) for x in range(ranks.x) for c in range(ranks.core)][1:]
        stats = add_wide([stats, *[ranks.loop_shift(stats, x=x, core=c) for x, c in steps]])
        stats = [stats, *[ranks.rows_shift(stats, high=h) for h in range(1, ranks.high)]]
        image_sums = [image_part[0, 0]]
        for x in range(1, ranks.x):
            image_sums.append(ranks.loop_shift(sent(image_part, (0, x)), x=-x))
        for low in range(1, ranks.low):
            got = [ranks.loop_shift(sent(image_part, (low, x)), x=-x) for x in range(1, ranks.x)]
            total = add_low([image_part[low, 0], *got], *totals)
            image_sums.append(ranks.rows_shift(total, low=-low))
        grad_text, done = finish(scale, text_feats, text_sums, flops=FIRST)
        grad_image, done = finish(scale, image_feats, image_sums, done)
        return grad_image, grad_text, mean_stats(devices * rows_dev, stats, done)

    rows_spec = P(("groups", "loop", "rows"), None)
    return jax.shard_map(
        shards,
        mesh=mesh,
        in_specs=(rows_spec, rows_spec, P(), P()),
        out_specs=(rows_spec, rows_spec, P("groups")),
        check_vma=False,
    )
```

```python
import functools

import jax
import jax.numpy as jnp
from jax import lax
from jax.experimental import pallas as pl
from jax.experimental.pallas import tpu as pltpu
from jax.sharding import PartitionSpec as P

EPSILON = 1e-06
IMAGE_TILE, TEXT_TILE = 8, 2
FIRST = 10**9
AHEAD = 12 * 10**9
VMEM = pl.BlockSpec(memory_space=pltpu.VMEM)
SMEM = pl.BlockSpec(memory_space=pltpu.SMEM)
PARAMS = pltpu.CompilerParams(vmem_limit_bytes=24 * 1024 * 1024)
ROW_DOT = (((1,), (1,)), ((), ()))
COL_DOT = (((0,), (0,)), ((), ()))
LOW, WIDE = jnp.bfloat16, jnp.float32


def array(shape, dtype):
    return jax.ShapeDtypeStruct(shape, dtype)


def call(kernel, outs, flops, *args, smem=0):
    nbytes = sum(a.size * a.dtype.itemsize for a in (*args, *outs))
    single = len(outs) == 1
    return pl.pallas_call(
        kernel,
        out_shape=outs[0] if single else tuple(outs),
        in_specs=[SMEM] * smem + [VMEM] * (len(args) - smem),
        out_specs=VMEM if single else tuple([VMEM] * len(outs)),
        compiler_params=PARAMS,
        cost_estimate=pl.CostEstimate(flops=flops, bytes_accessed=nbytes, transcendentals=0),
    )(*args)


def normalize_kernel(feats_ref, *refs):
    feats = feats_ref[...]
    inverse = lax.rsqrt(jnp.sum(feats * feats, axis=1, keepdims=True) + EPSILON)
    refs[-1][...] = (feats * inverse).astype(LOW)


def normalize(feats, *others):
    return call(normalize_kernel, [array(feats.shape, LOW)], 4 * feats.size, feats, *others)


def token_kernel(*refs):
    refs[-1][...] = jnp.zeros(refs[-1].shape, WIDE)


def token(*others, flops=0):
    return call(token_kernel, [array((8, 128), WIDE)], 1024 + flops, *others)


def joined(refs):
    return jnp.concatenate([r[...] for r in refs], axis=0)


def spread(value, refs):
    at = 0
    for ref in refs:
        rows = ref.shape[0]
        ref[...] = value[at : at + rows].astype(ref.dtype)
        at += rows


def score_kernel(own, n_image, n_text, *refs):
    scale_ref, bias_ref = refs[:2]
    texts = joined(refs[2 : 2 + n_text])
    images = joined(refs[2 + n_text : 2 + n_text + n_image])
    grad_ref, stats_ref = refs[-2:]
    scores = lax.dot_general(images, texts, ROW_DOT, preferred_element_type=WIDE)
    scaled = scale_ref[0] * scores
    logits = scaled + bias_ref[0]
    if own:
        row = lax.broadcasted_iota(jnp.int32, logits.shape, 0)
        col = lax.broadcasted_iota(jnp.int32, logits.shape, 1)
        sign = jnp.where((row == col) & (row < own), 1.0, -1.0).astype(WIDE)
    else:
        sign = jnp.full(logits.shape, -1.0, WIDE)
    against = -sign * logits
    small = jnp.exp(-jnp.abs(against))
    above = jnp.where(against >= 0, 1.0, small) / (1.0 + small)
    pair_grad = -sign * above
    loss = jnp.maximum(against, 0.0) + jnp.log1p(small)
    which = lax.broadcasted_iota(jnp.int32, stats_ref.shape, 0)
    stats_ref[...] = jnp.where(
        which == 0,
        jnp.sum(loss),
        jnp.where(which == 1, jnp.sum(pair_grad * scaled), jnp.sum(pair_grad)),
    )
    grad_ref[...] = pair_grad.astype(LOW)


def score_tile(own, scale, bias, images, texts, *others):
    rows_i, rows_t = sum(v.shape[0] for v in images), sum(v.shape[0] for v in texts)
    outs = [array((rows_i, rows_t), LOW), array((8, 128), WIDE)]
    kernel = functools.partial(score_kernel, own, len(images), len(texts))
    flops = 2 * rows_i * rows_t * images[0].shape[1]
    return call(kernel, outs, flops, scale, bias, *texts, *images, *others, smem=2)


def image_kernel(at, rows, n_text, n_out, grad_ref, *refs):
    texts = joined(refs[:n_text])
    spread(jnp.dot(grad_ref[at : at + rows], texts, preferred_element_type=WIDE), refs[-n_out:])


def image_tile(at, pair_grad, texts, outs, *others):
    rows = sum(out.shape[0] for out in outs)
    kernel = functools.partial(image_kernel, at, rows, len(texts), len(outs))
    flops = 2 * rows * pair_grad.shape[1] * texts[0].shape[1]
    got = call(kernel, outs, flops, pair_grad, *texts, *others)
    return list(got) if len(outs) > 1 else [got]


def text_kernel(n_image, n_out, grad_ref, *refs):
    images = joined(refs[:n_image])
    text_grad = lax.dot_general(grad_ref[...], images, COL_DOT, preferred_element_type=WIDE)
    spread(text_grad, refs[-n_out:])


def text_tile(pair_grad, images, outs, *others):
    kernel = functools.partial(text_kernel, len(images), len(outs))
    flops = 2 * pair_grad.size * images[0].shape[1]
    got = call(kernel, outs, flops, pair_grad, *images, *others)
    return list(got) if len(outs) > 1 else [got]


def added_up(parts):
    return add(parts[0].shape, WIDE, [(v, 0) for v in parts])


def block(ref, at, rows):
    return ref[...] if ref.shape[0] == rows else ref[at : at + rows]


def add_kernel(places, *refs):
    rows = refs[-1].shape[0]
    total = block(refs[0], places[0], rows).astype(WIDE)
    for ref, at in zip(refs[1:], places[1:]):
        total = total + block(ref, at, rows).astype(WIDE)
    refs[-1][...] = total.astype(refs[-1].dtype)


def add(shape, dtype, parts, *others):
    kernel = functools.partial(add_kernel, [at for _, at in parts])
    flops = len(parts) * shape[0] * shape[1]
    return call(kernel, [array(shape, dtype)], flops, *(v for v, _ in parts), *others)


def finish_kernel(places, scale_ref, feats_ref, *refs):
    feats = feats_ref[...]
    rows = feats.shape[0]
    inverse = lax.rsqrt(jnp.sum(feats * feats, axis=1, keepdims=True) + EPSILON)
    unit = feats * inverse
    total = block(refs[0], places[0], rows).astype(WIDE)
    for ref, at in zip(refs[1:], places[1:]):
        total = total + block(ref, at, rows).astype(WIDE)
    grad = scale_ref[0] * total
    refs[-2][...] = (grad - unit * jnp.sum(unit * grad, axis=1, keepdims=True)) * inverse
    refs[-1][...] = jnp.zeros(refs[-1].shape, WIDE)


def finish(scale, feats, parts, *others, flops=0):
    kernel = functools.partial(finish_kernel, [at for _, at in parts])
    outs = [array(feats.shape, WIDE), array((8, 128), WIDE)]
    args = [v for v, _ in parts]
    return call(kernel, outs, 10 * feats.size + flops, scale, feats, *args, *others, smem=1)


def mean_kernel(count, batch, *refs):
    total = refs[0][...]
    for ref in refs[1:count]:
        total = total + ref[...]
    total = total / batch
    for i in range(3):
        refs[-1][i] = total[i, 0]


def mean_stats(batch, parts, *others):
    return pl.pallas_call(
        functools.partial(mean_kernel, len(parts), float(batch)),
        out_shape=array((3,), WIDE),
        in_specs=[VMEM] * (len(parts) + len(others)),
        out_specs=SMEM,
        compiler_params=PARAMS,
    )(*parts, *others)


class Ranks:
    def __init__(self, mesh):
        loop, rows = mesh.shape["loop"], mesh.shape["rows"]
        core = 2 if loop % 2 == 0 else 1
        low = 2 if rows % 2 == 0 else 1
        self.x, self.core, self.high, self.low = loop // core, core, rows // low, low

    def loop_shift(self, value, x=0, core=0):
        pairs = []
        for a in range(self.x):
            for b in range(self.core):
                to = (a + x) % self.x * self.core + (b + core) % self.core
                pairs.append((a * self.core + b, to))
        return lax.ppermute(value, "loop", pairs)

    def rows_shift(self, value, high=0, low=0, keep=lambda distance: True):
        pairs = []
        for a in range(self.high):
            for b in range(self.low):
                to = (a + high) % self.high * self.low + (b + low) % self.low
                if keep(abs(a * self.low + b - to)):
                    pairs.append((a * self.low + b, to))
        return lax.ppermute(value, "rows", pairs)


def near(distance):
    return distance <= 1


def far(distance):
    return distance > 1


def solution(mesh):
    ranks = Ranks(mesh)
    devices = mesh.shape["loop"] * mesh.shape["rows"]

    def shards(image_feats, text_feats, log_scale, bias):
        rows_dev = image_feats.shape[0]
        scale = jnp.exp(log_scale)
        text_low = normalize(text_feats)
        image_low = normalize(image_feats, text_low)

        texts, halves = {0: text_low}, {}
        for high in range(1, ranks.high):
            halves[high] = [ranks.rows_shift(text_low, high, high, keep) for keep in (near, far)]
        order = token(*(h[0] for h in halves.values()))
        images = {(0, 0, 0): image_low}
        for low in range(1, ranks.low):
            images[low, 0, 0] = ranks.rows_shift(image_low, low=low)
        for low in range(ranks.low):
            for x in range(1, ranks.x):
                images[low, x, 0] = ranks.loop_shift(images[low, 0, 0], x=x)
        order = token(*(images[low, 0, 0] for low in range(ranks.low)), order)
        order = token(*(images[0, x, 0] for x in range(ranks.x)), order)
        for high, got in halves.items():
            texts[high] = add(text_low.shape, LOW, [(v, 0) for v in got], order)
        arrived = token(*texts.values(), order, flops=AHEAD)
        for low in range(ranks.low):
            for x in range(ranks.x):
                if low and x:
                    images[low, x, 0] = add(image_low.shape, LOW, [(images[low, x, 0], 0)], arrived)
                for core in range(1, ranks.core):
                    images[low, x, core] = ranks.loop_shift(images[low, x, 0], core=core)

        groups = [[(low, x, 0)] for low in range(ranks.low) for x in range(ranks.x)]
        for core in range(1, ranks.core):
            groups += [[(low, x, core) for x in range(ranks.x)] for low in range(ranks.low)]
        blocks = sum(len(g) for g in groups)
        if blocks > IMAGE_TILE or len(texts) > TEXT_TILE:
            groups = [[key] for g in groups for key in g]
        one_tile = blocks <= IMAGE_TILE and len(texts) <= TEXT_TILE
        per_tile = len(groups) if one_tile else IMAGE_TILE
        parts, text_parts, tiles, stats = {}, {}, [], None

        def added(store, key, value):
            store[key] = store[key] + value if key in store else value

        for i in range(0, len(groups), per_tile):
            some = groups[i : i + per_tile]
            held = [images[key] for g in some for key in g]
            outs = [
                array((len(g) * rows_dev, image_low.shape[1]), LOW if one_tile and g[0][2] else WIDE) for g in some
            ]
            for j in range(0, len(texts), TEXT_TILE):
                keys = list(texts)[j : j + TEXT_TILE]
                own = rows_dev if i == 0 and j == 0 else 0
                pair = [texts[k] for k in keys]
                pair_grad, tile_stats = score_tile(own, scale, bias, held, pair, arrived)
                tiles.append((keys, pair_grad, held, some, outs))
                stats = tile_stats if stats is None else stats + tile_stats

        def image_grads(wanted, *others):
            for keys, pair_grad, _, some, outs in tiles:
                chosen = [i for i, g in enumerate(some) if bool(g[0][2]) == wanted]
                if chosen:
                    at = sum(len(g) for g in some[: chosen[0]]) * rows_dev
                    got = image_tile(at, pair_grad, [texts[k] for k in keys], [outs[i] for i in chosen], *others)
                    for i, value in zip(chosen, got):
                        added(parts, tuple(some[i]), value)

        image_grads(True)
        for keys, pair_grad, held, _, _ in tiles:
            text_outs = [array(text_low.shape, LOW if one_tile and k else WIDE) for k in keys]
            for k, value in zip(keys, text_tile(pair_grad, held, text_outs)):
                added(text_parts, k, value)
        image_grads(False)
        stats = added_up([stats, *[ranks.loop_shift(stats, core=c) for c in range(1, ranks.core)]])
        stats = added_up([stats, *[ranks.loop_shift(stats, x=x) for x in range(1, ranks.x)]])
        for core in range(1, ranks.core):
            for low in reversed(range(ranks.low)):
                keys = [(low, x, core) for x in range(ranks.x)]
                if tuple(keys) not in parts:
                    parts[tuple(keys)] = jnp.concatenate([parts[(key,)].astype(LOW) for key in keys], axis=0)
        back = {
            (low, core): ranks.loop_shift(parts[tuple((low, x, core) for x in range(ranks.x))], core=-core)
            for low in reversed(range(ranks.low))
            for core in range(1, ranks.core)
        }

        def here(low, x):
            return [(parts[((low, x, 0),)], 0)] + [(back[low, c], x * rows_dev) for c in range(1, ranks.core)]

        shape = image_low.shape
        image_sums = here(0, 0)
        for low in range(1, ranks.low):
            got = [(ranks.loop_shift(add(shape, LOW, here(low, x)), x=-x), 0) for x in range(1, ranks.x)]
            image_sums.append((ranks.rows_shift(add(shape, LOW, here(low, 0) + got, stats), low=-low), 0))
        for x in range(1, ranks.x):
            image_sums.append((ranks.loop_shift(add(shape, LOW, here(0, x)), x=-x), 0))
        text_sums = [(text_parts[0], 0)]
        for high in range(1, ranks.high):
            text_sums.append((ranks.rows_shift(text_parts[high].astype(LOW), -high, -high), 0))
        steps = [(h, k) for h in range(ranks.high) for k in range(ranks.low)][1:]
        stats = [stats, *[ranks.rows_shift(stats, high=h, low=k) for h, k in steps]]
        grad_text, done = finish(scale, text_feats, text_sums, flops=FIRST)
        grad_image, done = finish(scale, image_feats, image_sums, done)
        return grad_image, grad_text, mean_stats(devices * rows_dev, stats, done)

    rows_spec = P(("groups", "loop", "rows"), None)
    return jax.shard_map(
        shards,
        mesh=mesh,
        in_specs=(rows_spec, rows_spec, P(), P()),
        out_specs=(rows_spec, rows_spec, P("groups")),
        check_vma=False,
    )
```

```python
import functools

import jax
import jax.numpy as jnp
from jax import lax
from jax.experimental import pallas as pl
from jax.experimental.pallas import tpu as pltpu
from jax.sharding import PartitionSpec as P

EPSILON = 1e-06
IMAGE_TILE, TEXT_TILE = 8, 2
FIRST = 10**9
AHEAD = 12 * 10**9
VMEM = pl.BlockSpec(memory_space=pltpu.VMEM)
SMEM = pl.BlockSpec(memory_space=pltpu.SMEM)
PARAMS = pltpu.CompilerParams(vmem_limit_bytes=24 * 1024 * 1024)
ROW_DOT = (((1,), (1,)), ((), ()))
COL_DOT = (((0,), (0,)), ((), ()))
LOW, WIDE = jnp.bfloat16, jnp.float32


def array(shape, dtype):
    return jax.ShapeDtypeStruct(shape, dtype)


def call(kernel, outs, flops, *args, smem=0):
    nbytes = sum(a.size * a.dtype.itemsize for a in (*args, *outs))
    single = len(outs) == 1
    return pl.pallas_call(
        kernel,
        out_shape=outs[0] if single else tuple(outs),
        in_specs=[SMEM] * smem + [VMEM] * (len(args) - smem),
        out_specs=VMEM if single else tuple([VMEM] * len(outs)),
        compiler_params=PARAMS,
        cost_estimate=pl.CostEstimate(flops=flops, bytes_accessed=nbytes, transcendentals=0),
    )(*args)


def normalize_kernel(feats_ref, *refs):
    feats = feats_ref[...]
    inverse = lax.rsqrt(jnp.sum(feats * feats, axis=1, keepdims=True) + EPSILON)
    refs[-1][...] = (feats * inverse).astype(LOW)


def normalize(feats, *others):
    return call(normalize_kernel, [array(feats.shape, LOW)], 4 * feats.size, feats, *others)


def token_kernel(*refs):
    refs[-1][...] = jnp.zeros(refs[-1].shape, WIDE)


def token(*others, flops=0, smem=0):
    return call(token_kernel, [array((8, 128), WIDE)], 1024 + flops, *others, smem=smem)


def joined(refs):
    return jnp.concatenate([r[...] for r in refs], axis=0)


def spread(value, refs):
    at = 0
    for ref in refs:
        rows = ref.shape[0]
        ref[...] = value[at : at + rows].astype(ref.dtype)
        at += rows


def score_kernel(own, n_image, n_text, *refs):
    scale_ref, bias_ref = refs[:2]
    texts = joined(refs[2 : 2 + n_text])
    images = joined(refs[2 + n_text : 2 + n_text + n_image])
    grad_ref, stats_ref = refs[-2:]
    scores = lax.dot_general(images, texts, ROW_DOT, preferred_element_type=WIDE)
    scaled = scale_ref[0] * scores
    logits = scaled + bias_ref[0]
    if own:
        row = lax.broadcasted_iota(jnp.int32, logits.shape, 0)
        col = lax.broadcasted_iota(jnp.int32, logits.shape, 1)
        sign = jnp.where((row == col) & (row < own), 1.0, -1.0).astype(WIDE)
    else:
        sign = jnp.full(logits.shape, -1.0, WIDE)
    against = -sign * logits
    small = jnp.exp(-jnp.abs(against))
    above = jnp.where(against >= 0, 1.0, small) / (1.0 + small)
    pair_grad = -sign * above
    loss = jnp.maximum(against, 0.0) + jnp.log1p(small)
    which = lax.broadcasted_iota(jnp.int32, stats_ref.shape, 0)
    stats_ref[...] = jnp.where(
        which == 0,
        jnp.sum(loss),
        jnp.where(which == 1, jnp.sum(pair_grad * scaled), jnp.sum(pair_grad)),
    )
    grad_ref[...] = pair_grad.astype(LOW)


def score_tile(own, scale, bias, images, texts, *others):
    rows_i, rows_t = sum(v.shape[0] for v in images), sum(v.shape[0] for v in texts)
    outs = [array((rows_i, rows_t), LOW), array((8, 128), WIDE)]
    kernel = functools.partial(score_kernel, own, len(images), len(texts))
    flops = 2 * rows_i * rows_t * images[0].shape[1]
    return call(kernel, outs, flops, scale, bias, *texts, *images, *others, smem=2)


def image_kernel(at, rows, n_grad, n_text, n_out, *refs):
    grads, texts = joined(refs[:n_grad])[at : at + rows], joined(refs[n_grad : n_grad + n_text])
    spread(jnp.dot(grads, texts, preferred_element_type=WIDE), refs[-n_out:])


def image_tile(at, pair_grads, texts, outs, *others):
    rows = sum(out.shape[0] for out in outs)
    kernel = functools.partial(image_kernel, at, rows, len(pair_grads), len(texts), len(outs))
    flops = 2 * rows * pair_grads[0].shape[1] * texts[0].shape[1]
    got = call(kernel, outs, flops, *pair_grads, *texts, *others)
    return list(got) if len(outs) > 1 else [got]


def text_kernel(n_grad, n_image, n_out, *refs):
    grads, images = joined(refs[:n_grad]), joined(refs[n_grad : n_grad + n_image])
    text_grad = lax.dot_general(grads, images, COL_DOT, preferred_element_type=WIDE)
    spread(text_grad, refs[-n_out:])


def text_tile(pair_grads, images, outs, *others):
    kernel = functools.partial(text_kernel, len(pair_grads), len(images), len(outs))
    flops = 2 * sum(v.size for v in pair_grads) * images[0].shape[1]
    got = call(kernel, outs, flops, *pair_grads, *images, *others)
    return list(got) if len(outs) > 1 else [got]


def added_up(parts):
    return add(parts[0].shape, WIDE, [(v, 0) for v in parts])


def block(ref, at, rows):
    return ref[...] if ref.shape[0] == rows else ref[at : at + rows]


def add_kernel(places, *refs):
    rows = refs[-1].shape[0]
    total = block(refs[0], places[0], rows).astype(WIDE)
    for ref, at in zip(refs[1:], places[1:]):
        total = total + block(ref, at, rows).astype(WIDE)
    refs[-1][...] = total.astype(refs[-1].dtype)


def add(shape, dtype, parts, *others):
    kernel = functools.partial(add_kernel, [at for _, at in parts])
    flops = len(parts) * shape[0] * shape[1]
    return call(kernel, [array(shape, dtype)], flops, *(v for v, _ in parts), *others)


def finish_kernel(places, scale_ref, feats_ref, *refs):
    feats = feats_ref[...]
    rows = feats.shape[0]
    inverse = lax.rsqrt(jnp.sum(feats * feats, axis=1, keepdims=True) + EPSILON)
    unit = feats * inverse
    total = block(refs[0], places[0], rows).astype(WIDE)
    for ref, at in zip(refs[1:], places[1:]):
        total = total + block(ref, at, rows).astype(WIDE)
    grad = scale_ref[0] * total
    refs[-2][...] = (grad - unit * jnp.sum(unit * grad, axis=1, keepdims=True)) * inverse
    refs[-1][...] = jnp.zeros(refs[-1].shape, WIDE)


def finish(scale, feats, parts, *others, flops=0):
    kernel = functools.partial(finish_kernel, [at for _, at in parts])
    outs = [array(feats.shape, WIDE), array((8, 128), WIDE)]
    args = [v for v, _ in parts]
    return call(kernel, outs, 10 * feats.size + flops, scale, feats, *args, *others, smem=1)


def mean_kernel(count, batch, *refs):
    total = refs[0][...]
    for ref in refs[1:count]:
        total = total + ref[...]
    total = total / batch
    for i in range(3):
        refs[-1][i] = total[i, 0]


def mean_stats(batch, parts, *others):
    return pl.pallas_call(
        functools.partial(mean_kernel, len(parts), float(batch)),
        out_shape=array((3,), WIDE),
        in_specs=[VMEM] * (len(parts) + len(others)),
        out_specs=SMEM,
        compiler_params=PARAMS,
    )(*parts, *others)


class Ranks:
    def __init__(self, mesh):
        loop, rows = mesh.shape["loop"], mesh.shape["rows"]
        core = 2 if loop % 2 == 0 else 1
        low = 2 if rows % 2 == 0 else 1
        self.x, self.core, self.high, self.low = loop // core, core, rows // low, low

    def loop_shift(self, value, x=0, core=0):
        pairs = []
        for a in range(self.x):
            for b in range(self.core):
                to = (a + x) % self.x * self.core + (b + core) % self.core
                pairs.append((a * self.core + b, to))
        return lax.ppermute(value, "loop", pairs)

    def rows_shift(self, value, high=0, low=0, keep=lambda distance: True):
        pairs = []
        for a in range(self.high):
            for b in range(self.low):
                to = (a + high) % self.high * self.low + (b + low) % self.low
                if keep(abs(a * self.low + b - to)):
                    pairs.append((a * self.low + b, to))
        return lax.ppermute(value, "rows", pairs)


def near(distance):
    return distance <= 1


def far(distance):
    return distance > 1


def solution(mesh):
    ranks = Ranks(mesh)
    devices = mesh.shape["loop"] * mesh.shape["rows"]

    def shards(image_feats, text_feats, log_scale, bias):
        rows_dev = image_feats.shape[0]
        scale = jnp.exp(log_scale)
        text_low = normalize(text_feats)
        image_low = normalize(image_feats, text_low)

        texts, halves = {0: text_low}, {}
        for high in range(1, ranks.high):
            halves[high] = [ranks.rows_shift(text_low, high, high, keep) for keep in (near, far)]
        order = token(*(h[0] for h in halves.values()))
        images = {(0, 0, 0): image_low}
        for low in range(1, ranks.low):
            images[low, 0, 0] = ranks.rows_shift(image_low, low=low)
        for low in range(ranks.low):
            for x in range(1, ranks.x):
                images[low, x, 0] = ranks.loop_shift(images[low, 0, 0], x=x)
        order = token(*(images[low, 0, 0] for low in range(ranks.low)), order)
        order = token(scale, bias, *(images[0, x, 0] for x in range(ranks.x)), order, smem=2)
        for high, got in halves.items():
            texts[high] = add(text_low.shape, LOW, [(v, 0) for v in got], order)
        arrived = token(*texts.values(), order, flops=AHEAD)
        for low in range(ranks.low):
            for x in range(ranks.x):
                if low and x:
                    images[low, x, 0] = add(image_low.shape, LOW, [(images[low, x, 0], 0)], arrived)
                for core in range(1, ranks.core):
                    images[low, x, core] = ranks.loop_shift(images[low, x, 0], core=core)

        groups = [[(low, x, 0)] for low in range(ranks.low) for x in range(ranks.x)]
        for core in range(1, ranks.core):
            groups += [[(low, x, core) for x in range(ranks.x)] for low in range(ranks.low)]
        blocks = sum(len(g) for g in groups)
        if blocks > IMAGE_TILE or len(texts) > TEXT_TILE:
            groups = [[key] for g in groups for key in g]
        one_tile = blocks <= IMAGE_TILE and len(texts) <= TEXT_TILE
        per_tile = len(groups) if one_tile else IMAGE_TILE
        parts, text_parts, tiles, stats = {}, {}, [], []

        def added(store, key, value):
            store[key] = store[key] + value if key in store else value

        for i in range(0, len(groups), per_tile):
            some = groups[i : i + per_tile]
            held = [images[key] for g in some for key in g]
            outs = [
                array((len(g) * rows_dev, image_low.shape[1]), LOW if one_tile and g[0][2] else WIDE) for g in some
            ]
            for j in range(0, len(texts), TEXT_TILE):
                keys = list(texts)[j : j + TEXT_TILE]
                own = rows_dev if i == 0 and j == 0 else 0
                pair = [texts[k] for k in keys]
                cuts = [held[:-1], held[-1:]] if len(held) > 1 else [held]
                got = [score_tile(own if not n else 0, scale, bias, c, pair, arrived) for n, c in enumerate(cuts)]
                tiles.append((keys, [g for g, _ in got], held, some, outs))
                stats += [s for _, s in got]

        def image_grads(wanted, *others):
            for keys, pair_grad, _, some, outs in tiles:
                chosen = [i for i, g in enumerate(some) if bool(g[0][2]) == wanted]
                if chosen:
                    at = sum(len(g) for g in some[: chosen[0]]) * rows_dev
                    got = image_tile(at, pair_grad, [texts[k] for k in keys], [outs[i] for i in chosen], *others)
                    for i, value in zip(chosen, got):
                        added(parts, tuple(some[i]), value)

        image_grads(True)
        for keys, pair_grad, held, _, _ in tiles:
            text_outs = [array(text_low.shape, LOW if one_tile and k else WIDE) for k in keys]
            for k, value in zip(keys, text_tile(pair_grad, held, text_outs)):
                added(text_parts, k, value)
        image_grads(False)
        stats = added_up(stats)
        stats = added_up([stats, *[ranks.loop_shift(stats, core=c) for c in range(1, ranks.core)]])
        stats = added_up([stats, *[ranks.loop_shift(stats, x=x) for x in range(1, ranks.x)]])
        for core in range(1, ranks.core):
            for low in reversed(range(ranks.low)):
                keys = [(low, x, core) for x in range(ranks.x)]
                if tuple(keys) not in parts:
                    parts[tuple(keys)] = jnp.concatenate([parts[(key,)].astype(LOW) for key in keys], axis=0)
        back = {
            (low, core): ranks.loop_shift(parts[tuple((low, x, core) for x in range(ranks.x))], core=-core)
            for low in reversed(range(ranks.low))
            for core in range(1, ranks.core)
        }

        def here(low, x):
            return [(parts[((low, x, 0),)], 0)] + [(back[low, c], x * rows_dev) for c in range(1, ranks.core)]

        shape = image_low.shape
        image_sums, ahead = here(0, 0), []
        for low in range(1, ranks.low):
            got = [
                (ranks.loop_shift(add(shape, LOW, here(low, x), *text_parts.values()), x=-x), 0)
                for x in range(1, ranks.x)
            ]
            ahead.append(ranks.rows_shift(add(shape, LOW, here(low, 0) + got, stats), low=-low))
        for x in range(1, ranks.x):
            image_sums.append((ranks.loop_shift(add(shape, LOW, here(0, x)), x=-x), 0))
        image_sums += [(v, 0) for v in ahead]
        text_sums = [(text_parts[0], 0)]
        for high in range(1, ranks.high):
            text_sums.append((ranks.rows_shift(text_parts[high].astype(LOW), -high, -high), 0))
        steps = [(h, k) for h in range(ranks.high) for k in range(ranks.low)][1:]
        stats = [stats, *[ranks.rows_shift(stats, high=h, low=k) for h, k in steps]]
        grad_text, done = finish(scale, text_feats, text_sums, flops=FIRST)
        grad_image, done = finish(scale, image_feats, image_sums, token(done, *ahead))
        return grad_image, grad_text, mean_stats(devices * rows_dev, stats, done)

    rows_spec = P(("groups", "loop", "rows"), None)
    return jax.shard_map(
        shards,
        mesh=mesh,
        in_specs=(rows_spec, rows_spec, P(), P()),
        out_specs=(rows_spec, rows_spec, P("groups")),
        check_vma=False,
    )
```

```python
import functools

import jax
import jax.numpy as jnp
from jax import lax
from jax.experimental import pallas as pl
from jax.experimental.pallas import tpu as pltpu
from jax.sharding import PartitionSpec as P

EPSILON = 1e-06
IMAGE_TILE, TEXT_TILE = 8, 2
FIRST = 10**9
AHEAD = 12 * 10**9
VMEM = pl.BlockSpec(memory_space=pltpu.VMEM)
SMEM = pl.BlockSpec(memory_space=pltpu.SMEM)
PARAMS = pltpu.CompilerParams(vmem_limit_bytes=24 * 1024 * 1024)
ROW_DOT = (((1,), (1,)), ((), ()))
COL_DOT = (((0,), (0,)), ((), ()))
LOW, WIDE = jnp.bfloat16, jnp.float32


def array(shape, dtype):
    return jax.ShapeDtypeStruct(shape, dtype)


def call(kernel, outs, flops, *args, smem=0):
    nbytes = sum(a.size * a.dtype.itemsize for a in (*args, *outs))
    single = len(outs) == 1
    return pl.pallas_call(
        kernel,
        out_shape=outs[0] if single else tuple(outs),
        in_specs=[SMEM] * smem + [VMEM] * (len(args) - smem),
        out_specs=VMEM if single else tuple([VMEM] * len(outs)),
        compiler_params=PARAMS,
        cost_estimate=pl.CostEstimate(flops=flops, bytes_accessed=nbytes, transcendentals=0),
    )(*args)


def normalize_kernel(feats_ref, *refs):
    feats = feats_ref[...]
    inverse = lax.rsqrt(jnp.sum(feats * feats, axis=1, keepdims=True) + EPSILON)
    refs[-1][...] = (feats * inverse).astype(LOW)


def normalize(feats, *others):
    return call(normalize_kernel, [array(feats.shape, LOW)], 4 * feats.size, feats, *others)


def token_kernel(*refs):
    refs[-1][...] = jnp.zeros(refs[-1].shape, WIDE)


def token(*others, flops=0, smem=0):
    return call(token_kernel, [array((8, 128), WIDE)], 1024 + flops, *others, smem=smem)


def joined(refs):
    return jnp.concatenate([r[...] for r in refs], axis=0)


def spread(value, refs):
    at = 0
    for ref in refs:
        rows = ref.shape[0]
        ref[...] = value[at : at + rows].astype(ref.dtype)
        at += rows


def score_kernel(own, n_image, n_text, *refs):
    scale_ref, bias_ref = refs[:2]
    texts = joined(refs[2 : 2 + n_text])
    images = joined(refs[2 + n_text : 2 + n_text + n_image])
    grad_ref, stats_ref = refs[-2:]
    scores = lax.dot_general(images, texts, ROW_DOT, preferred_element_type=WIDE)
    scaled = scale_ref[0] * scores
    logits = scaled + bias_ref[0]
    grown = jnp.exp(logits)
    pair_grad = grown / (1.0 + grown)
    joint = grown
    for _ in range(2):
        half = joint.shape[0] // 2
        if half % 8 == 0:
            upper, lower = joint[:half], joint[half:]
            joint = upper + lower + upper * lower
    loss = jnp.sum(jnp.log1p(joint))
    if own:
        row = lax.broadcasted_iota(jnp.int32, (own, own), 0)
        col = lax.broadcasted_iota(jnp.int32, (own, own), 1)
        same = jnp.where(row == col, 1.0, 0.0).astype(WIDE)
        loss = loss - jnp.sum(same * logits[:own, :own])
        top = pair_grad[:own, :own] - same
        if pair_grad.shape[1] > own:
            top = jnp.concatenate([top, pair_grad[:own, own:]], axis=1)
        pair_grad = jnp.concatenate([top, pair_grad[own:]], axis=0) if pair_grad.shape[0] > own else top
    which = lax.broadcasted_iota(jnp.int32, stats_ref.shape, 0)
    stats_ref[...] = jnp.where(
        which == 0,
        loss,
        jnp.where(which == 1, jnp.sum(pair_grad * scaled), jnp.sum(pair_grad)),
    )
    grad_ref[...] = pair_grad.astype(LOW)


def score_tile(own, scale, bias, images, texts, *others):
    rows_i, rows_t = sum(v.shape[0] for v in images), sum(v.shape[0] for v in texts)
    outs = [array((rows_i, rows_t), LOW), array((8, 128), WIDE)]
    kernel = functools.partial(score_kernel, own, len(images), len(texts))
    flops = 2 * rows_i * rows_t * images[0].shape[1]
    return call(kernel, outs, flops, scale, bias, *texts, *images, *others, smem=2)


def image_kernel(at, rows, n_grad, n_text, n_out, *refs):
    grads, texts = joined(refs[:n_grad])[at : at + rows], joined(refs[n_grad : n_grad + n_text])
    spread(jnp.dot(grads, texts, preferred_element_type=WIDE), refs[-n_out:])


def image_tile(at, pair_grads, texts, outs, *others):
    rows = sum(out.shape[0] for out in outs)
    kernel = functools.partial(image_kernel, at, rows, len(pair_grads), len(texts), len(outs))
    flops = 2 * rows * pair_grads[0].shape[1] * texts[0].shape[1]
    got = call(kernel, outs, flops, *pair_grads, *texts, *others)
    return list(got) if len(outs) > 1 else [got]


def text_kernel(n_grad, n_image, n_out, *refs):
    grads, images = joined(refs[:n_grad]), joined(refs[n_grad : n_grad + n_image])
    text_grad = lax.dot_general(grads, images, COL_DOT, preferred_element_type=WIDE)
    spread(text_grad, refs[-n_out:])


def text_tile(pair_grads, images, outs, *others):
    kernel = functools.partial(text_kernel, len(pair_grads), len(images), len(outs))
    flops = 2 * sum(v.size for v in pair_grads) * images[0].shape[1]
    got = call(kernel, outs, flops, *pair_grads, *images, *others)
    return list(got) if len(outs) > 1 else [got]


def added_up(parts):
    return add(parts[0].shape, WIDE, [(v, 0) for v in parts])


def block(ref, at, rows):
    return ref[...] if ref.shape[0] == rows else ref[at : at + rows]


def add_kernel(places, *refs):
    rows = refs[-1].shape[0]
    total = block(refs[0], places[0], rows).astype(WIDE)
    for ref, at in zip(refs[1:], places[1:]):
        total = total + block(ref, at, rows).astype(WIDE)
    refs[-1][...] = total.astype(refs[-1].dtype)


def add(shape, dtype, parts, *others):
    kernel = functools.partial(add_kernel, [at for _, at in parts])
    flops = len(parts) * shape[0] * shape[1]
    return call(kernel, [array(shape, dtype)], flops, *(v for v, _ in parts), *others)


def finish_kernel(places, scale_ref, feats_ref, *refs):
    feats = feats_ref[...]
    rows = feats.shape[0]
    inverse = lax.rsqrt(jnp.sum(feats * feats, axis=1, keepdims=True) + EPSILON)
    unit = feats * inverse
    total = block(refs[0], places[0], rows).astype(WIDE)
    for ref, at in zip(refs[1:], places[1:]):
        total = total + block(ref, at, rows).astype(WIDE)
    grad = scale_ref[0] * total
    refs[-2][...] = (grad - unit * jnp.sum(unit * grad, axis=1, keepdims=True)) * inverse
    refs[-1][...] = jnp.zeros(refs[-1].shape, WIDE)


def finish(scale, feats, parts, *others, flops=0):
    kernel = functools.partial(finish_kernel, [at for _, at in parts])
    outs = [array(feats.shape, WIDE), array((8, 128), WIDE)]
    args = [v for v, _ in parts]
    return call(kernel, outs, 10 * feats.size + flops, scale, feats, *args, *others, smem=1)


def mean_kernel(count, batch, *refs):
    total = refs[0][...]
    for ref in refs[1:count]:
        total = total + ref[...]
    total = total / batch
    for i in range(3):
        refs[-1][i] = total[i, 0]


def mean_stats(batch, parts, *others):
    return pl.pallas_call(
        functools.partial(mean_kernel, len(parts), float(batch)),
        out_shape=array((3,), WIDE),
        in_specs=[VMEM] * (len(parts) + len(others)),
        out_specs=SMEM,
        compiler_params=PARAMS,
    )(*parts, *others)


class Ranks:
    def __init__(self, mesh):
        loop, rows = mesh.shape["loop"], mesh.shape["rows"]
        core = 2 if loop % 2 == 0 else 1
        low = 2 if rows % 2 == 0 else 1
        self.x, self.core, self.high, self.low = loop // core, core, rows // low, low

    def loop_shift(self, value, x=0, core=0):
        pairs = []
        for a in range(self.x):
            for b in range(self.core):
                to = (a + x) % self.x * self.core + (b + core) % self.core
                pairs.append((a * self.core + b, to))
        return lax.ppermute(value, "loop", pairs)

    def rows_shift(self, value, high=0, low=0, keep=lambda distance: True):
        pairs = []
        for a in range(self.high):
            for b in range(self.low):
                to = (a + high) % self.high * self.low + (b + low) % self.low
                if keep(abs(a * self.low + b - to)):
                    pairs.append((a * self.low + b, to))
        return lax.ppermute(value, "rows", pairs)


def near(distance):
    return distance <= 1


def far(distance):
    return distance > 1


def solution(mesh):
    ranks = Ranks(mesh)
    devices = mesh.shape["loop"] * mesh.shape["rows"]

    def shards(image_feats, text_feats, log_scale, bias):
        rows_dev = image_feats.shape[0]
        scale = jnp.exp(log_scale)
        text_low = normalize(text_feats)
        image_low = normalize(image_feats, text_low)

        texts, halves = {0: text_low}, {}
        for high in range(1, ranks.high):
            halves[high] = [ranks.rows_shift(text_low, high, high, keep) for keep in (near, far)]
        order = token(*(h[0] for h in halves.values()))
        images = {(0, 0, 0): image_low}
        for low in range(1, ranks.low):
            images[low, 0, 0] = ranks.rows_shift(image_low, low=low)
        for low in range(ranks.low):
            for x in range(1, ranks.x):
                images[low, x, 0] = ranks.loop_shift(images[low, 0, 0], x=x)
        order = token(*(images[low, 0, 0] for low in range(ranks.low)), order)
        order = token(scale, bias, *(images[0, x, 0] for x in range(ranks.x)), order, smem=2)
        for high, got in halves.items():
            texts[high] = add(text_low.shape, LOW, [(v, 0) for v in got], order)
        arrived = token(*texts.values(), order, flops=AHEAD)
        for low in range(ranks.low):
            for x in range(ranks.x):
                if low and x:
                    images[low, x, 0] = add(image_low.shape, LOW, [(images[low, x, 0], 0)], arrived)
                for core in range(1, ranks.core):
                    images[low, x, core] = ranks.loop_shift(images[low, x, 0], core=core)

        groups = [[(low, x, 0)] for low in range(ranks.low) for x in range(ranks.x)]
        for core in range(1, ranks.core):
            groups += [[(low, x, core) for x in range(ranks.x)] for low in range(ranks.low)]
        blocks = sum(len(g) for g in groups)
        if blocks > IMAGE_TILE or len(texts) > TEXT_TILE:
            groups = [[key] for g in groups for key in g]
        one_tile = blocks <= IMAGE_TILE and len(texts) <= TEXT_TILE
        per_tile = len(groups) if one_tile else IMAGE_TILE
        parts, text_parts, tiles, stats = {}, {}, [], []

        def added(store, key, value):
            store[key] = store[key] + value if key in store else value

        for i in range(0, len(groups), per_tile):
            some = groups[i : i + per_tile]
            held = [images[key] for g in some for key in g]
            outs = [
                array((len(g) * rows_dev, image_low.shape[1]), LOW if one_tile and g[0][2] else WIDE) for g in some
            ]
            for j in range(0, len(texts), TEXT_TILE):
                keys = list(texts)[j : j + TEXT_TILE]
                own = rows_dev if i == 0 and j == 0 else 0
                pair = [texts[k] for k in keys]
                cuts = [held[:-1], held[-1:]] if len(held) > 1 else [held]
                got = [score_tile(own if not n else 0, scale, bias, c, pair, arrived) for n, c in enumerate(cuts)]
                tiles.append((keys, [g for g, _ in got], held, some, outs))
                stats += [s for _, s in got]

        def image_grads(wanted, *others):
            for keys, pair_grad, _, some, outs in tiles:
                chosen = [i for i, g in enumerate(some) if bool(g[0][2]) == wanted]
                if chosen:
                    at = sum(len(g) for g in some[: chosen[0]]) * rows_dev
                    got = image_tile(at, pair_grad, [texts[k] for k in keys], [outs[i] for i in chosen], *others)
                    for i, value in zip(chosen, got):
                        added(parts, tuple(some[i]), value)

        image_grads(True)
        for keys, pair_grad, held, _, _ in tiles:
            text_outs = [array(text_low.shape, LOW if one_tile and k else WIDE) for k in keys]
            for k, value in zip(keys, text_tile(pair_grad, held, text_outs)):
                added(text_parts, k, value)
        image_grads(False)
        stats = added_up(stats)
        stats = added_up([stats, *[ranks.loop_shift(stats, core=c) for c in range(1, ranks.core)]])
        stats = added_up([stats, *[ranks.loop_shift(stats, x=x) for x in range(1, ranks.x)]])
        for core in range(1, ranks.core):
            for low in reversed(range(ranks.low)):
                keys = [(low, x, core) for x in range(ranks.x)]
                if tuple(keys) not in parts:
                    parts[tuple(keys)] = jnp.concatenate([parts[(key,)].astype(LOW) for key in keys], axis=0)
        back = {
            (low, core): ranks.loop_shift(parts[tuple((low, x, core) for x in range(ranks.x))], core=-core)
            for low in reversed(range(ranks.low))
            for core in range(1, ranks.core)
        }

        def here(low, x):
            return [(parts[((low, x, 0),)], 0)] + [(back[low, c], x * rows_dev) for c in range(1, ranks.core)]

        shape = image_low.shape
        image_sums, ahead = here(0, 0), []
        for low in range(1, ranks.low):
            got = [
                (ranks.loop_shift(add(shape, LOW, here(low, x), *text_parts.values()), x=-x), 0)
                for x in range(1, ranks.x)
            ]
            ahead.append(ranks.rows_shift(add(shape, LOW, here(low, 0) + got, stats), low=-low))
        for x in range(1, ranks.x):
            image_sums.append((ranks.loop_shift(add(shape, LOW, here(0, x)), x=-x), 0))
        image_sums += [(v, 0) for v in ahead]
        text_sums = [(text_parts[0], 0)]
        for high in range(1, ranks.high):
            text_sums.append((ranks.rows_shift(text_parts[high].astype(LOW), -high, -high), 0))
        steps = [(h, k) for h in range(ranks.high) for k in range(ranks.low)][1:]
        stats = [stats, *[ranks.rows_shift(stats, high=h, low=k) for h, k in steps]]
        grad_text, done = finish(scale, text_feats, text_sums, flops=FIRST)
        grad_image, done = finish(scale, image_feats, image_sums, token(done, *ahead))
        return grad_image, grad_text, mean_stats(devices * rows_dev, stats, done)

    rows_spec = P(("groups", "loop", "rows"), None)
    return jax.shard_map(
        shards,
        mesh=mesh,
        in_specs=(rows_spec, rows_spec, P(), P()),
        out_specs=(rows_spec, rows_spec, P("groups")),
        check_vma=False,
    )
```

```python
import functools

import jax
import jax.numpy as jnp
from jax import lax
from jax.experimental import pallas as pl
from jax.experimental.pallas import tpu as pltpu
from jax.sharding import PartitionSpec as P

EPSILON = 1e-06
IMAGE_TILE, TEXT_TILE = 8, 2
FIRST = 10**9
AHEAD = 12 * 10**9
VMEM = pl.BlockSpec(memory_space=pltpu.VMEM)
SMEM = pl.BlockSpec(memory_space=pltpu.SMEM)
PARAMS = pltpu.CompilerParams(vmem_limit_bytes=24 * 1024 * 1024)
ROW_DOT = (((1,), (1,)), ((), ()))
COL_DOT = (((0,), (0,)), ((), ()))
LOW, WIDE = jnp.bfloat16, jnp.float32


def array(shape, dtype):
    return jax.ShapeDtypeStruct(shape, dtype)


def call(kernel, outs, flops, *args, smem=0):
    nbytes = sum(a.size * a.dtype.itemsize for a in (*args, *outs))
    single = len(outs) == 1
    return pl.pallas_call(
        kernel,
        out_shape=outs[0] if single else tuple(outs),
        in_specs=[SMEM] * smem + [VMEM] * (len(args) - smem),
        out_specs=VMEM if single else tuple([VMEM] * len(outs)),
        compiler_params=PARAMS,
        cost_estimate=pl.CostEstimate(flops=flops, bytes_accessed=nbytes, transcendentals=0),
    )(*args)


def normalize_kernel(feats_ref, *refs):
    feats = feats_ref[...]
    inverse = lax.rsqrt(jnp.sum(feats * feats, axis=1, keepdims=True) + EPSILON)
    refs[-1][...] = (feats * inverse).astype(LOW)


def normalize(feats, *others):
    return call(normalize_kernel, [array(feats.shape, LOW)], 4 * feats.size, feats, *others)


def token_kernel(*refs):
    refs[-1][...] = jnp.zeros(refs[-1].shape, WIDE)


def token(*others, flops=0, smem=0):
    return call(token_kernel, [array((8, 128), WIDE)], 1024 + flops, *others, smem=smem)


def joined(refs):
    return jnp.concatenate([r[...] for r in refs], axis=0)


def spread(value, refs):
    at = 0
    for ref in refs:
        rows = ref.shape[0]
        ref[...] = value[at : at + rows].astype(ref.dtype)
        at += rows


def score_kernel(own, n_image, n_text, *refs):
    scale_ref, bias_ref = refs[:2]
    texts = joined(refs[2 : 2 + n_text])
    images = joined(refs[2 + n_text : 2 + n_text + n_image])
    grad_ref, stats_ref = refs[-2:]
    scores = lax.dot_general(images, texts, ROW_DOT, preferred_element_type=WIDE)
    scaled = scale_ref[0] * scores
    logits = scaled + bias_ref[0]
    grown = jnp.exp(logits)
    pair_grad = grown / (1.0 + grown)
    joint = grown
    for _ in range(2):
        half = joint.shape[0] // 2
        if half % 8 == 0:
            upper, lower = joint[:half], joint[half:]
            joint = upper + lower + upper * lower
    loss = jnp.sum(jnp.log1p(joint))
    if own:
        row = lax.broadcasted_iota(jnp.int32, (own, own), 0)
        col = lax.broadcasted_iota(jnp.int32, (own, own), 1)
        same = jnp.where(row == col, 1.0, 0.0).astype(WIDE)
        loss = loss - jnp.sum(same * logits[:own, :own])
        top = pair_grad[:own, :own] - same
        if pair_grad.shape[1] > own:
            top = jnp.concatenate([top, pair_grad[:own, own:]], axis=1)
        pair_grad = jnp.concatenate([top, pair_grad[own:]], axis=0) if pair_grad.shape[0] > own else top
    which = lax.broadcasted_iota(jnp.int32, stats_ref.shape, 0)
    stats_ref[...] = jnp.where(
        which == 0,
        loss,
        jnp.where(which == 1, jnp.sum(pair_grad * scaled), jnp.sum(pair_grad)),
    )
    grad_ref[...] = pair_grad.astype(LOW)


def score_tile(own, scale, bias, images, texts, *others):
    rows_i, rows_t = sum(v.shape[0] for v in images), sum(v.shape[0] for v in texts)
    outs = [array((rows_i, rows_t), LOW), array((8, 128), WIDE)]
    kernel = functools.partial(score_kernel, own, len(images), len(texts))
    flops = 2 * rows_i * rows_t * images[0].shape[1]
    return call(kernel, outs, flops, scale, bias, *texts, *images, *others, smem=2)


def image_kernel(at, rows, n_grad, n_text, n_out, *refs):
    grads, texts = joined(refs[:n_grad])[at : at + rows], joined(refs[n_grad : n_grad + n_text])
    spread(jnp.dot(grads, texts, preferred_element_type=WIDE), refs[-n_out:])


def image_tile(at, pair_grads, texts, outs, *others):
    rows = sum(out.shape[0] for out in outs)
    kernel = functools.partial(image_kernel, at, rows, len(pair_grads), len(texts), len(outs))
    flops = 2 * rows * pair_grads[0].shape[1] * texts[0].shape[1]
    got = call(kernel, outs, flops, *pair_grads, *texts, *others)
    return list(got) if len(outs) > 1 else [got]


def text_kernel(n_grad, n_image, n_out, *refs):
    grads, images = joined(refs[:n_grad]), joined(refs[n_grad : n_grad + n_image])
    text_grad = lax.dot_general(grads, images, COL_DOT, preferred_element_type=WIDE)
    spread(text_grad, refs[-n_out:])


def text_tile(pair_grads, images, outs, *others):
    kernel = functools.partial(text_kernel, len(pair_grads), len(images), len(outs))
    flops = 2 * sum(v.size for v in pair_grads) * images[0].shape[1]
    got = call(kernel, outs, flops, *pair_grads, *images, *others)
    return list(got) if len(outs) > 1 else [got]


def added_up(parts):
    return add(parts[0].shape, WIDE, [(v, 0) for v in parts])


def block(ref, at, rows):
    return ref[...] if ref.shape[0] == rows else ref[at : at + rows]


def add_kernel(places, *refs):
    rows = refs[-1].shape[0]
    total = block(refs[0], places[0], rows).astype(WIDE)
    for ref, at in zip(refs[1:], places[1:]):
        total = total + block(ref, at, rows).astype(WIDE)
    refs[-1][...] = total.astype(refs[-1].dtype)


def add(shape, dtype, parts, *others):
    kernel = functools.partial(add_kernel, [at for _, at in parts])
    flops = len(parts) * shape[0] * shape[1]
    return call(kernel, [array(shape, dtype)], flops, *(v for v, _ in parts), *others)


def finish_kernel(places, scale_ref, feats_ref, *refs):
    feats = feats_ref[...]
    rows = feats.shape[0]
    inverse = lax.rsqrt(jnp.sum(feats * feats, axis=1, keepdims=True) + EPSILON)
    unit = feats * inverse
    total = block(refs[0], places[0], rows).astype(WIDE)
    for ref, at in zip(refs[1:], places[1:]):
        total = total + block(ref, at, rows).astype(WIDE)
    grad = scale_ref[0] * total
    refs[-2][...] = (grad - unit * jnp.sum(unit * grad, axis=1, keepdims=True)) * inverse
    refs[-1][...] = jnp.zeros(refs[-1].shape, WIDE)


def finish(scale, feats, parts, *others, flops=0):
    kernel = functools.partial(finish_kernel, [at for _, at in parts])
    outs = [array(feats.shape, WIDE), array((8, 128), WIDE)]
    args = [v for v, _ in parts]
    return call(kernel, outs, 10 * feats.size + flops, scale, feats, *args, *others, smem=1)


def mean_kernel(count, batch, *refs):
    total = refs[0][...]
    for ref in refs[1:count]:
        total = total + ref[...]
    total = total / batch
    for i in range(3):
        refs[-1][i] = total[i, 0]


def mean_stats(batch, parts, *others):
    return pl.pallas_call(
        functools.partial(mean_kernel, len(parts), float(batch)),
        out_shape=array((3,), WIDE),
        in_specs=[VMEM] * (len(parts) + len(others)),
        out_specs=SMEM,
        compiler_params=PARAMS,
    )(*parts, *others)


class Ranks:
    def __init__(self, mesh):
        loop, rows = mesh.shape["loop"], mesh.shape["rows"]
        core = 2 if loop % 2 == 0 else 1
        low = 2 if rows % 2 == 0 else 1
        self.x, self.core, self.high, self.low = loop // core, core, rows // low, low

    def loop_shift(self, value, x=0, core=0):
        pairs = []
        for a in range(self.x):
            for b in range(self.core):
                to = (a + x) % self.x * self.core + (b + core) % self.core
                pairs.append((a * self.core + b, to))
        return lax.ppermute(value, "loop", pairs)

    def rows_shift(self, value, high=0, low=0, keep=lambda distance: True):
        pairs = []
        for a in range(self.high):
            for b in range(self.low):
                to = (a + high) % self.high * self.low + (b + low) % self.low
                if keep(abs(a * self.low + b - to)):
                    pairs.append((a * self.low + b, to))
        return lax.ppermute(value, "rows", pairs)


def near(distance):
    return distance <= 1


def far(distance):
    return distance > 1


def solution(mesh):
    ranks = Ranks(mesh)
    devices = mesh.shape["loop"] * mesh.shape["rows"]

    def shards(image_feats, text_feats, log_scale, bias):
        rows_dev = image_feats.shape[0]
        scale = jnp.exp(log_scale)
        text_low = normalize(text_feats)
        image_low = normalize(image_feats, text_low)

        texts, halves = {0: text_low}, {}
        for high in range(1, ranks.high):
            halves[high] = [ranks.rows_shift(text_low, high, high, keep) for keep in (near, far)]
        order = token(*(h[0] for h in halves.values()))
        images = {(0, 0, 0): image_low}
        for low in range(1, ranks.low):
            images[low, 0, 0] = ranks.rows_shift(image_low, low=low)
        for low in range(ranks.low):
            for x in range(1, ranks.x):
                images[low, x, 0] = ranks.loop_shift(images[low, 0, 0], x=x)
        order = token(*(images[low, 0, 0] for low in range(ranks.low)), order)
        order = token(scale, bias, *(images[0, x, 0] for x in range(ranks.x)), order, smem=2)
        for high, got in halves.items():
            texts[high] = add(text_low.shape, LOW, [(v, 0) for v in got], order)
        arrived = token(*texts.values(), order, flops=AHEAD)
        for low in range(ranks.low):
            for x in range(ranks.x):
                if low and x:
                    images[low, x, 0] = add(image_low.shape, LOW, [(images[low, x, 0], 0)], arrived)
                for core in range(1, ranks.core):
                    images[low, x, core] = ranks.loop_shift(images[low, x, 0], core=core)

        groups = [[(low, x, 0)] for low in range(ranks.low) for x in range(ranks.x)]
        for core in range(1, ranks.core):
            groups += [[(low, x, core) for x in range(ranks.x)] for low in range(ranks.low)]
        blocks = sum(len(g) for g in groups)
        if blocks > IMAGE_TILE or len(texts) > TEXT_TILE:
            groups = [[key] for g in groups for key in g]
        one_tile = blocks <= IMAGE_TILE and len(texts) <= TEXT_TILE
        per_tile = len(groups) if one_tile else IMAGE_TILE
        parts, text_parts, tiles, stats = {}, {}, [], []

        def added(store, key, value):
            store[key] = store[key] + value if key in store else value

        for i in range(0, len(groups), per_tile):
            some = groups[i : i + per_tile]
            held = [images[key] for g in some for key in g]
            outs = [
                array((len(g) * rows_dev, image_low.shape[1]), LOW if one_tile and g[0][2] else WIDE) for g in some
            ]
            for j in range(0, len(texts), TEXT_TILE):
                keys = list(texts)[j : j + TEXT_TILE]
                own = rows_dev if i == 0 and j == 0 else 0
                pair = [texts[k] for k in keys]
                cuts = [held[:-1], held[-1:]] if len(held) > 1 else [held]
                got = [score_tile(own if not n else 0, scale, bias, c, pair, arrived) for n, c in enumerate(cuts)]
                tiles.append((keys, [g for g, _ in got], held, some, outs))
                stats += [s for _, s in got]

        def image_grads(wanted, *others):
            for keys, pair_grad, _, some, outs in tiles:
                chosen = [i for i, g in enumerate(some) if bool(g[0][2]) == wanted]
                if chosen:
                    at = sum(len(g) for g in some[: chosen[0]]) * rows_dev
                    got = image_tile(at, pair_grad, [texts[k] for k in keys], [outs[i] for i in chosen], *others)
                    for i, value in zip(chosen, got):
                        added(parts, tuple(some[i]), value)

        image_grads(True)
        for keys, pair_grad, held, _, _ in tiles:
            text_outs = [array(text_low.shape, LOW if one_tile and k else WIDE) for k in keys]
            for k, value in zip(keys, text_tile(pair_grad, held, text_outs)):
                added(text_parts, k, value)
        image_grads(False)
        stats = added_up(stats)
        stats = added_up([stats, *[ranks.loop_shift(stats, core=c) for c in range(1, ranks.core)]])
        stats = added_up([stats, *[ranks.loop_shift(stats, x=x) for x in range(1, ranks.x)]])
        for core in range(1, ranks.core):
            for low in reversed(range(ranks.low)):
                keys = [(low, x, core) for x in range(ranks.x)]
                if tuple(keys) not in parts:
                    parts[tuple(keys)] = jnp.concatenate([parts[(key,)].astype(LOW) for key in keys], axis=0)
        back = {
            (low, core): ranks.loop_shift(parts[tuple((low, x, core) for x in range(ranks.x))], core=-core)
            for low in reversed(range(ranks.low))
            for core in range(1, ranks.core)
        }

        def here(low, x):
            return [(parts[((low, x, 0),)], 0)] + [(back[low, c], x * rows_dev) for c in range(1, ranks.core)]

        shape = image_low.shape
        image_sums, ahead = here(0, 0), []
        for low in range(1, ranks.low):
            got = [
                (ranks.loop_shift(add(shape, LOW, here(low, x), *text_parts.values()), x=-x), 0)
                for x in range(1, ranks.x)
            ]
            ahead.append(ranks.rows_shift(add(shape, LOW, here(low, 0) + got), low=-low))
        for x in range(1, ranks.x):
            image_sums.append((ranks.loop_shift(add(shape, LOW, here(0, x), stats), x=-x), 0))
        image_sums += [(v, 0) for v in ahead]
        text_sums = [(text_parts[0], 0)]
        for high in range(1, ranks.high):
            text_sums.append((ranks.rows_shift(text_parts[high].astype(LOW), -high, -high), 0))
        steps = [(h, k) for h in range(ranks.high) for k in range(ranks.low)][1:]
        stats = [stats, *[ranks.rows_shift(stats, high=h, low=k) for h, k in steps]]
        grad_text, done = finish(scale, text_feats, text_sums, flops=FIRST)
        grad_image, done = finish(scale, image_feats, image_sums, token(done, *ahead))
        return grad_image, grad_text, mean_stats(devices * rows_dev, stats, done)

    rows_spec = P(("groups", "loop", "rows"), None)
    return jax.shard_map(
        shards,
        mesh=mesh,
        in_specs=(rows_spec, rows_spec, P(), P()),
        out_specs=(rows_spec, rows_spec, P("groups")),
        check_vma=False,
    )
```
